32 devices in a mesh: segment: 2 (over x), row: 4 (over y, core), col: 4 (over z).
Axes of the slice: x: 2, y: 2, z: 4, core: 2. Of those that a mesh axis runs over, the one named last changes fastest.
Arguments:
- dosage: float32 [2048, 6144], P(('segment', 'col'), 'row'), may hold values from 0 to 2, as said below
- missing: int32 [2048, 6144], P(('segment', 'col'), 'row'), may hold values 0 or 1
- residuals: bfloat16 [6144, 256], P('row'), may hold values from -6 to 6
- global_grm: bfloat16 [6144, 6144], P('row', 'col'), may hold values from -1 to 2
- seg_counts: int32 [6], replicated, may hold values from 1 to 1024, 2048 in all
Outputs:
- scores: bfloat16 [6, 6144, 256], P(None, ('row', 'col'), 'segment')
The draws below stay inside these ranges and needn't reach their ends.
Inputs may be any that keep to these rules, and one draw needn't show every extreme that they name: `dosage`: imputed alternative-allele dosages. 1 marks a missing genotype. `seg_counts`: SNP counts of the 6 segments, laid end to end over the 2048 variants; they sum to 2048 and the largest is exactly 1024.
All inputs are finite; a program needn't handle non-finite values. No bound on the sum of `missing` on one device may be relied on, other than what follows from the above.
Results may differ from the reference program's by a relative error of at most 0.0053.
Values may be sent and summed in bfloat16 or wider, within the bound.
No kernel may reach another device: no remote copies, remote signals or barrier semaphores. Data moves between devices by JAX's collectives and lax.ppermute only.
A program may use at most 320 MiB of HBM per device.

```python
import math
import jax
import jax.numpy as jnp
import numpy as np
from jax import lax

TILE = 1536
RESCOLS = 256
MOST = 1024
SEGMENTS = 6
VARS = 2048
SAMPLES = 6144
N_SEGMENT = 2
N_ROW = 4


def draw_dosage(key, part):
    key_base, key_one, key_two, key_mix = jax.random.split(key, 4)
    base_freq = jax.random.uniform(key_base, (VARS, 1), jnp.float32, 0.05, 0.31)
    sample_pos = lax.broadcasted_iota(jnp.int32, (1, SAMPLES), 1).astype(jnp.float32)
    freq = base_freq * (1.0 + 2.0 * sample_pos / SAMPLES)
    first_allele = (jax.random.uniform(key_one, (VARS, SAMPLES), jnp.float32) < freq).astype(jnp.float32)
    second_allele = (jax.random.uniform(key_two, (VARS, SAMPLES), jnp.float32) < freq).astype(jnp.float32)
    genotype = first_allele + second_allele
    certainty = jax.random.uniform(key_mix, (VARS, SAMPLES), jnp.float32, 0.6, 1.0)
    return 2.0 * freq * (1.0 - certainty) + genotype * certainty


def draw_global_grm(key, part):
    spread_vals = jnp.clip(0.2 * jax.random.normal(key, (SAMPLES, SAMPLES), jnp.float32), -1.0, 1.0)
    on_diagonal = (lax.broadcasted_iota(jnp.int32, (SAMPLES, SAMPLES), 0) == lax.broadcasted_iota(jnp.int32, (SAMPLES, SAMPLES), 1)).astype(jnp.float32)
    return (spread_vals + on_diagonal).astype(jnp.bfloat16)


def set_ends(entries, own_key, smallest, top_value):
    longest = entries.shape.index(max(entries.shape))
    spots = []
    for shift in (0, 1):
        where = [jax.random.randint(jax.random.fold_in(own_key, axis), (), 0, length) for axis, length in enumerate(entries.shape)]
        where[longest] = (where[longest] + shift) % entries.shape[longest]
        spots.append(tuple(where))
    return entries.at[spots[0]].set(smallest).at[spots[1]].set(top_value)


def block_levels(own_key, extent, cuts, least, high):
    def one(position, shards_of):
        steps = jax.random.uniform(jax.random.fold_in(jax.random.fold_in(own_key, 6), position), (shards_of,), jnp.float32, least / len(cuts), high / len(cuts))
        return jnp.repeat(jnp.exp(steps), extent[position] // shards_of).reshape((-1,) + (1,) * (len(extent) - position - 1))

    level = one(*cuts[0])
    for cut in cuts[1:]:
        level = level * one(*cut)
    return level


def profile(count, total, most, slope):
    weights = [(1 << 20) // math.isqrt(standing ** slope) + 1 for standing in range(2, count + 1)]
    spare, given = total - most - (count - 1), [1] * (count - 1)
    while spare > 0:
        candidates = [i for i in range(count - 1) if given[i] < most]
        mass, budget = sum([weights[i] for i in candidates]), spare
        for i in candidates:
            more = min(most - given[i], max(1, budget * weights[i] // mass), spare)
            given[i] = given[i] + more
            spare = spare - more
    return np.array([most] + given)


def uneven(stream_key, number_of, total, bound, slope):
    if number_of == 2:
        one = jax.random.randint(stream_key, (), max(1, total - bound), min(bound, total - 1) + 1)
        return jnp.stack([one, total - one])
    tallies = jnp.asarray(profile(number_of, total, bound, slope), jnp.int32)
    couples = (number_of - 1) // 2
    source_of, receiver = tallies[1:1 + 2 * couples:2], tallies[2:2 + 2 * couples:2]
    slack = jnp.minimum(source_of - 1, bound - receiver)
    moved = jax.random.randint(jax.random.fold_in(stream_key, 1), (couples,), 0, 1 << 20) % (slack + 1)
    tallies = tallies.at[1:1 + 2 * couples:2].set(source_of - moved).at[2:2 + 2 * couples:2].set(receiver + moved)
    return tallies[jax.random.permutation(jax.random.fold_in(stream_key, 2), number_of)]


def bell_draw(stream_key, extent, width, most, shards=(), kind=jnp.bfloat16):
    entries = width * jax.random.normal(stream_key, extent, jnp.float32)
    if shards:
        entries = entries * block_levels(stream_key, extent, shards, -0.22, 0.18)
    return jnp.clip(entries, -most, most).astype(kind)


def setup_inputs(seed: int = 0) -> dict:
    arg_keys = jax.random.split(jax.random.key(seed), 6)
    return {
        "dosage": draw_dosage(jax.random.fold_in(arg_keys[5], 71), 0),
        "missing": set_ends((jax.random.randint(arg_keys[1], (VARS, SAMPLES), 0, 20) < 1).astype(jnp.int32), jax.random.fold_in(arg_keys[1], 1), 0, 1),
        "residuals": bell_draw(arg_keys[2], (SAMPLES, RESCOLS), 1.0, 6.0, ((0, 4),)),
        "global_grm": draw_global_grm(jax.random.fold_in(arg_keys[5], 71), 0),
        "seg_counts": uneven(arg_keys[4], SEGMENTS, VARS, MOST, 2).astype(jnp.int32),
    }


def reference(dosage, missing, residuals, global_grm, seg_counts):
    observed = (1 - missing).astype(jnp.float32)
    dosage_f = dosage.astype(jnp.float32)
    alt_count = lax.optimization_barrier(jnp.sum(dosage_f * observed, axis=1))
    obs_count = lax.optimization_barrier(jnp.sum(observed, axis=1))
    allele_freq = (alt_count + 1.0) / (2.0 * obs_count + 2.0)
    allele_spread = jnp.sqrt(2.0 * allele_freq * (1.0 - allele_freq))
    standard = (observed * (dosage_f - 2.0 * allele_freq[:, None]) / allele_spread[:, None]).astype(jnp.bfloat16)
    seg_starts = (jnp.cumsum(seg_counts) - seg_counts).astype(jnp.int32)
    shard_vars = VARS // N_SEGMENT
    res_f = residuals.astype(jnp.float32)
    outputs = []
    for segment_num in range(SEGMENTS):
        seg_start = seg_starts[segment_num]
        seg_count = seg_counts[segment_num]
        windows = []
        for shard_num in range(N_SEGMENT):
            lower = jnp.clip(seg_start, shard_num * shard_vars, (shard_num + 1) * shard_vars).astype(jnp.int32)
            upper = jnp.clip(seg_start + seg_count, shard_num * shard_vars, (shard_num + 1) * shard_vars).astype(jnp.int32)
            first_row = jnp.minimum(lower, VARS - MOST).astype(jnp.int32)
            window = lax.dynamic_slice_in_dim(standard, first_row, MOST, 0).astype(jnp.float32)
            var_index = first_row + jnp.arange(MOST, dtype=jnp.int32)
            keep_mask = (var_index >= lower) & (var_index < upper)
            windows.append(jnp.where(keep_mask[:, None], window, jnp.zeros_like(window)))

        def tile_rows(tile_num, windows=windows, seg_count=seg_count):
            row_start = (tile_num * TILE).astype(jnp.int32)
            grm_rows = lax.dynamic_slice_in_dim(global_grm, row_start, TILE, 0).astype(jnp.float32)
            total = jnp.zeros((TILE, RESCOLS), jnp.float32)
            for window in windows:
                rows_part = lax.dynamic_slice_in_dim(window, row_start, TILE, 1)
                local_gram = jnp.dot(rows_part.T, window, precision=lax.Precision.HIGHEST)
                hadamard = (local_gram / seg_count.astype(jnp.float32) * grm_rows).astype(jnp.bfloat16)
                total = total + jnp.dot(hadamard.astype(jnp.float32), res_f, precision=lax.Precision.HIGHEST)
            return total.astype(jnp.bfloat16)
        blocks = lax.map(tile_rows, jnp.arange(N_ROW, dtype=jnp.int32))
        outputs.append(blocks.reshape(SAMPLES, RESCOLS))
    return jnp.stack(outputs)
```

```python
import functools

import jax
import jax.numpy as jnp
from jax import lax
from jax.experimental import pallas as pl
from jax.experimental.pallas import tpu as pltpu
from jax.sharding import PartitionSpec as P

BLOCK = 256
COL_TILE = 512


def spread(piece, row, col, n_row, n_col):
    have = piece
    bit = n_row // 2
    while bit:
        pairs = [
            (r * n_col + c, (r ^ bit) * n_col + c)
            for c in range(n_col)
            for r in range(n_row)
            if (r ^ c) & (2 * bit - 1) == 0
        ]
        got = lax.ppermute(have, ("row", "col"), pairs)
        have = jnp.where(((row ^ col) & (2 * bit - 1)) == bit, got, have)
        bit //= 2
    return have


def slot_kernel(shift, n, segments, info, inverse, *refs):
    rows, cols = refs[:n], refs[n : 2 * n]
    grm, res, own_out, send_out = refs[2 * n : 2 * n + 4]
    row_buf, col_buf, left_buf, grm_buf, res_buf, total, sems = refs[2 * n + 4 :]
    chunk, variants = row_buf.shape
    tile = col_buf.shape[0]
    share = variants // n
    col_tile = min(COL_TILE, tile)
    half = own_out.shape[2]
    col = info[2 * segments]
    first = pl.multiple_of(lax.rem(col + n - shift, n) * chunk, chunk)
    copies = []
    for s in range(n):
        at = pl.multiple_of(lax.rem(col + n - s, n) * share, share)
        copies.append(
            pltpu.make_async_copy(
                rows[s].at[pl.ds(first, chunk), :], row_buf.at[:, pl.ds(at, share)], sems.at[2 * s]
            )
        )
        copies.append(
            pltpu.make_async_copy(cols[s], col_buf.at[:, pl.ds(at, share)], sems.at[2 * s + 1])
        )
    copies.append(pltpu.make_async_copy(grm.at[pl.ds(first, chunk), :], grm_buf, sems.at[2 * n]))
    copies.append(pltpu.make_async_copy(res, res_buf, sems.at[2 * n + 1]))
    for copy in copies:
        copy.start()
    for copy in copies:
        copy.wait()

    def segment(s, carry):
        lower, upper = info[s], info[segments + s]
        first_block = lower // BLOCK
        blocks = (upper + BLOCK - 1) // BLOCK - first_block
        start = pl.multiple_of(first_block * BLOCK, BLOCK)

        @pl.when(upper <= lower)
        def _():
            own_out[s] = jnp.zeros(own_out.shape[1:], own_out.dtype)
            send_out[s] = jnp.zeros(send_out.shape[1:], send_out.dtype)

        for m in range(1, variants // BLOCK + 1):

            @pl.when((upper > lower) & (blocks == m))
            def _(m=m):
                depth = m * BLOCK
                index = start + lax.broadcasted_iota(jnp.int32, (chunk, depth), 1)
                left = row_buf[:, pl.ds(start, depth)]
                left_buf[:, :depth] = jnp.where(
                    (index >= lower) & (index < upper), left, jnp.zeros_like(left)
                )
                for j in range(tile // col_tile):
                    span = slice(j * col_tile, (j + 1) * col_tile)
                    gram = lax.dot_general(
                        left_buf[:, :depth],
                        col_buf[span, pl.ds(start, depth)],
                        (((1,), (1,)), ((), ())),
                        preferred_element_type=jnp.float32,
                    )
                    hadamard = (gram * grm_buf[:, span].astype(jnp.float32)).astype(jnp.bfloat16)
                    part = jnp.dot(hadamard, res_buf[span, :], preferred_element_type=jnp.float32)
                    if j == 0:
                        total[...] = part
                    else:
                        total[...] += part
                scores = total[...] * inverse[s]
                own_out[s] = scores[:, :half]
                send_out[s] = scores[:, half:].astype(send_out.dtype)

        return carry

    lax.fori_loop(0, segments, segment, 0)


def slot(shift, info, inverse, rows, cols, grm, res, segments, half):
    n = len(rows)
    tile, share = rows[0].shape
    chunk, variants = tile // n, share * n
    width = res.shape[1]
    any_spec = pl.BlockSpec(memory_space=pl.ANY)
    smem = pl.BlockSpec(memory_space=pltpu.SMEM)
    vmem = pl.BlockSpec(memory_space=pltpu.VMEM)
    return pl.pallas_call(
        functools.partial(slot_kernel, shift, n, segments),
        out_shape=(
            jax.ShapeDtypeStruct((segments, chunk, half), jnp.float32),
            jax.ShapeDtypeStruct((segments, chunk, width - half), jnp.bfloat16),
        ),
        in_specs=[smem, smem] + [any_spec] * (2 * n + 2),
        out_specs=(vmem, vmem),
        scratch_shapes=[
            pltpu.VMEM((chunk, variants), jnp.bfloat16),
            pltpu.VMEM((tile, variants), jnp.bfloat16),
            pltpu.VMEM((chunk, variants), jnp.bfloat16),
            pltpu.VMEM((chunk, tile), jnp.bfloat16),
            pltpu.VMEM((tile, width), jnp.bfloat16),
            pltpu.VMEM((chunk, width), jnp.float32),
            pltpu.SemaphoreType.DMA((2 * n + 2,)),
        ],
        compiler_params=pltpu.CompilerParams(vmem_limit_bytes=40 << 20),
        cost_estimate=pl.CostEstimate(
            flops=2 * chunk * tile * (variants + 4 * width),
            bytes_accessed=tile * variants * 2 + chunk * tile * 2 + tile * width * 2,
            transcendentals=0,
        ),
    )(info, inverse, *rows, *cols, grm, res)


def shards(dosage, missing, residuals, global_grm, seg_counts):
    n_seg, n_row, n_col = (lax.axis_size(a) for a in ("segment", "row", "col"))
    group, row, col = (lax.axis_index(a) for a in ("segment", "row", "col"))
    segments = seg_counts.shape[0]
    share, tile = dosage.shape
    width = residuals.shape[1]
    half = width // n_seg
    half_vars = share * n_col

    observed = (1 - missing).astype(jnp.float32)
    alt_local = jnp.sum(dosage * observed, axis=1)
    obs_local = jnp.sum(observed, axis=1)
    alt_total, obs_total = lax.psum((alt_local, obs_local), "row")
    allele_freq = (alt_total + 1.0) / (2.0 * obs_total + 2.0)
    allele_spread = jnp.sqrt(2.0 * allele_freq * (1.0 - allele_freq))
    standard = (observed * (dosage - 2.0 * allele_freq[:, None]) / allele_spread[:, None]).astype(
        jnp.bfloat16
    )

    seg_starts = jnp.cumsum(seg_counts) - seg_counts
    lower = jnp.clip(seg_starts - group * half_vars, 0, half_vars)
    upper = jnp.clip(seg_starts + seg_counts - group * half_vars, 0, half_vars)
    info = jnp.concatenate([lower, upper, col[None]]).astype(jnp.int32)
    inverse = 1.0 / seg_counts.astype(jnp.float32)

    parts = residuals.reshape(tile, n_seg, half)
    res = spread(jnp.roll(parts, -group, axis=1).reshape(tile, width), row, col, n_row, n_col)

    ring = [(i, (i + 1) % n_col) for i in range(n_col)]
    rows = [standard.T]
    for _ in range(n_col - 1):
        rows.append(lax.ppermute(rows[-1], "col", ring))
    cols = [spread(piece, row, col, n_row, n_col) for piece in rows]

    carried = None
    for k in range(1, n_col + 1):
        own, send = slot(k, info, inverse, rows, cols, global_grm, res, segments, half)
        got = own
        for j in range(1, n_seg):
            mine = send[:, :, (j - 1) * half : j * half]
            got = got + lax.ppermute(
                mine, "segment", [(i, (i + j) % n_seg) for i in range(n_seg)]
            ).astype(jnp.float32)
        if carried is not None:
            got = got + carried.astype(jnp.float32)
        got = got.astype(jnp.bfloat16)
        carried = lax.ppermute(got, "col", ring) if k < n_col else got
    return carried


def solution(mesh):
    placed = (
        P(("segment", "col"), "row"),
        P(("segment", "col"), "row"),
        P("row", None),
        P("row", "col"),
        P(),
    )
    return jax.shard_map(
        shards,
        mesh=mesh,
        in_specs=placed,
        out_specs=P(None, ("row", "col"), "segment"),
        check_vma=False,
    )
```

```python
import functools

import jax
import jax.numpy as jnp
from jax import lax
from jax.experimental import pallas as pl
from jax.experimental.pallas import tpu as pltpu
from jax.sharding import PartitionSpec as P

COL_TILE = 512
LAST_PARTS = 2


def in_vmem(x):
    return pltpu.with_memory_space_constraint(x, pltpu.VMEM)


def count_kernel(dosage, missing, turned, sums):
    share, tile = dosage.shape
    step = min(512, tile)
    alt = jnp.zeros((1, share), jnp.float32)
    obs = jnp.zeros((1, share), jnp.float32)
    for j in range(tile // step):
        span = slice(j * step, (j + 1) * step)
        coded = jnp.where(missing[:, span] == 0, dosage[:, span], -1.0).T
        turned[span, :] = coded
        seen = coded >= 0.0
        alt += jnp.sum(jnp.where(seen, coded, 0.0), axis=0, keepdims=True)
        obs += jnp.sum(jnp.where(seen, 1.0, 0.0), axis=0, keepdims=True)
    sums[...] = jnp.concatenate([alt, obs, jnp.zeros((6, share), jnp.float32)], axis=0)


def count(dosage, missing):
    share, tile = dosage.shape
    vmem = pl.BlockSpec(memory_space=pltpu.VMEM)
    return pl.pallas_call(
        count_kernel,
        out_shape=(
            jax.ShapeDtypeStruct((tile, share), jnp.float32),
            jax.ShapeDtypeStruct((8, share), jnp.float32),
        ),
        in_specs=[vmem, vmem],
        out_specs=(vmem, vmem),
        compiler_params=pltpu.CompilerParams(vmem_limit_bytes=24 << 20),
    )(dosage, missing)


def standard_kernel(turned, sums, out):
    tile, share = turned.shape
    step = min(256, tile)
    freq = (sums[0:1, :] + 1.0) / (2.0 * sums[1:2, :] + 2.0)
    centre = 2.0 * freq
    scale = 1.0 / jnp.sqrt(2.0 * freq * (1.0 - freq))
    for j in range(tile // step):
        span = slice(j * step, (j + 1) * step)
        coded = turned[span, :]
        out[span, :] = jnp.where(coded >= 0.0, (coded - centre) * scale, 0.0).astype(out.dtype)


def standardise(turned, sums):
    vmem = pl.BlockSpec(memory_space=pltpu.VMEM)
    return pl.pallas_call(
        standard_kernel,
        out_shape=jax.ShapeDtypeStruct(turned.shape, jnp.bfloat16),
        in_specs=[vmem, vmem],
        out_specs=vmem,
        compiler_params=pltpu.CompilerParams(vmem_limit_bytes=24 << 20),
    )(in_vmem(turned), in_vmem(sums))


def slot_kernel(shift, n, places, info, inverse, row_all, col_all, grm, res, *refs):
    own_out, send_out, left_buf, total = refs
    _, tile, share = row_all.shape
    chunk = tile // n
    col_tile = min(COL_TILE, tile)
    half = own_out.shape[2]
    col = info[2 * places]
    first = pl.multiple_of(lax.rem(col + n - shift, n) * chunk, chunk)

    def segment(s, carry):
        lower, upper = info[s], info[places + s]
        first_piece = lower // share
        pieces = (upper + share - 1) // share - first_piece

        @pl.when(upper <= lower)
        def _():
            own_out[s] = jnp.zeros(own_out.shape[1:], own_out.dtype)
            send_out[s] = jnp.zeros(send_out.shape[1:], send_out.dtype)

        for m in range(1, n + 1):

            @pl.when((upper > lower) & (pieces == m))
            def _(m=m):
                lies = [lax.rem(col + n - first_piece - i, n) for i in range(m)]
                for i in range(m):
                    index = (first_piece + i) * share + lax.broadcasted_iota(
                        jnp.int32, (chunk, share), 1
                    )
                    left = row_all[lies[i], pl.ds(first, chunk), :]
                    left_buf[i] = jnp.where(
                        (index >= lower) & (index < upper), left, jnp.zeros_like(left)
                    )
                scale = inverse[s]
                for j in range(tile // col_tile):
                    span = slice(j * col_tile, (j + 1) * col_tile)
                    gram = None
                    for i in range(m):
                        part = lax.dot_general(
                            left_buf[i],
                            col_all[lies[i], span, :],
                            (((1,), (1,)), ((), ())),
                            preferred_element_type=jnp.float32,
                        )
                        gram = part if gram is None else gram + part
                    grm_part = grm[pl.ds(first, chunk), span].astype(jnp.float32)
                    hadamard = (gram * scale * grm_part).astype(jnp.bfloat16)
                    part = jnp.dot(hadamard, res[span, :], preferred_element_type=jnp.float32)
                    if j == 0:
                        total[...] = part
                    else:
                        total[...] += part
                own_out[s] = total[:, :half]
                send_out[s] = total[:, half:].astype(send_out.dtype)

        return carry

    lax.fori_loop(0, places, segment, 0)


def slot(shift, info, inverse, row_all, col_all, grm, res):
    n, tile, share = row_all.shape
    places = inverse.shape[0]
    chunk = tile // n
    width = res.shape[1]
    half = width // 2
    smem = pl.BlockSpec(memory_space=pltpu.SMEM)
    vmem = pl.BlockSpec(memory_space=pltpu.VMEM)
    return pl.pallas_call(
        functools.partial(slot_kernel, shift, n, places),
        out_shape=(
            jax.ShapeDtypeStruct((places, chunk, half), jnp.float32),
            jax.ShapeDtypeStruct((places, chunk, half), jnp.bfloat16),
        ),
        in_specs=[smem, smem, vmem, vmem, vmem, vmem],
        out_specs=(vmem, vmem),
        scratch_shapes=[
            pltpu.VMEM((n, chunk, share), jnp.bfloat16),
            pltpu.VMEM((chunk, width), jnp.float32),
        ],
        compiler_params=pltpu.CompilerParams(vmem_limit_bytes=24 << 20),
        cost_estimate=pl.CostEstimate(
            flops=2 * chunk * tile * (n * share + places * width),
            bytes_accessed=tile * n * share * 2 + chunk * tile * 2 + tile * width * 2,
            transcendentals=0,
        ),
    )(info, inverse, in_vmem(row_all), in_vmem(col_all), in_vmem(grm), in_vmem(res))


def shards(dosage, missing, residuals, global_grm, seg_counts):
    n_seg, n_row, n_col = (lax.axis_size(a) for a in ("segment", "row", "col"))
    assert n_seg == 2 and n_row == n_col
    group, row, col = (lax.axis_index(a) for a in ("segment", "row", "col"))
    segments = seg_counts.shape[0]
    share, tile = dosage.shape
    width = residuals.shape[1]
    half = width // 2
    half_vars = share * n_col
    bits = [1 << b for b in range(n_row.bit_length() - 1)]

    def spread(piece):
        have = piece
        for bit in reversed(bits):
            pairs = [
                (r * n_col + c, (r ^ bit) * n_col + c)
                for c in range(n_col)
                for r in range(n_row)
                if (r ^ c) & (2 * bit - 1) == 0
            ]
            got = lax.ppermute(have, ("row", "col"), pairs)
            have = jnp.where(((row ^ col) & (2 * bit - 1)) == bit, got, have)
        return have

    turned, sums = count(dosage, missing)
    for bit in bits:
        sums = sums + lax.ppermute(sums, "row", [(r, r ^ bit) for r in range(n_row)])
    standard = standardise(turned, sums)

    parts = residuals.reshape(tile, 2, half)
    res = spread(jnp.where(group == 0, parts, parts[:, ::-1]).reshape(tile, width))

    ring = [(i, (i + 1) % n_col) for i in range(n_col)]
    rows = [standard]
    for _ in range(n_col - 2):
        rows.append(lax.ppermute(rows[-1], "col", ring))
    part = tile // LAST_PARTS
    rows += [
        lax.ppermute(rows[n_col - 2][i * part : (i + 1) * part], "col", ring)
        for i in range(LAST_PARTS)
    ]
    cols = [spread(piece) for piece in rows]
    row_all = jnp.concatenate(rows, axis=0).reshape(n_col, tile, share)
    col_all = jnp.concatenate(cols, axis=0).reshape(n_col, tile, share)

    seg_starts = jnp.cumsum(seg_counts) - seg_counts
    lower = jnp.clip(seg_starts - group * half_vars, 0, half_vars)
    upper = jnp.clip(seg_starts + seg_counts - group * half_vars, 0, half_vars)
    inverse = 1.0 / seg_counts.astype(jnp.float32)
    end = jnp.where(group == 0, 0, segments - 1)

    def chosen(x, a):
        if a:
            return jnp.stack([x[end], x[segments - 2]])
        return x[1 : segments - 2]

    infos = [
        jnp.concatenate([chosen(lower, a), chosen(upper, a), col[None]]).astype(jnp.int32)
        for a in (True, False)
    ]
    inverses = [chosen(inverse, a) for a in (True, False)]

    swap = [(0, 1), (1, 0)]
    carried = [None, None]
    for k in range(1, n_col + 1):
        for a in range(2):
            own, send = slot(k, infos[a], inverses[a], row_all, col_all, global_grm, res)
            got = lax.ppermute(send, "segment", swap).astype(jnp.float32)
            if a == 0:
                got = jnp.concatenate([own[:1], own[1:] + got[1:], got[:1]], axis=0)
            else:
                got = own + got
            if carried[a] is not None:
                got = got + carried[a].astype(jnp.float32)
            got = got.astype(jnp.bfloat16)
            carried[a] = lax.ppermute(got, "col", ring) if k < n_col else got
    ends, middle = carried
    ends = jnp.where(group == 0, ends, ends[::-1])
    return jnp.concatenate([ends[:1], middle, ends[1:]], axis=0)


def solution(mesh):
    placed = (
        P(("segment", "col"), "row"),
        P(("segment", "col"), "row"),
        P("row", None),
        P("row", "col"),
        P(),
    )
    return jax.shard_map(
        shards,
        mesh=mesh,
        in_specs=placed,
        out_specs=P(None, ("row", "col"), "segment"),
        check_vma=False,
    )
```

```python
import functools

import jax
import jax.numpy as jnp
from jax import lax
from jax.experimental import pallas as pl
from jax.experimental.pallas import tpu as pltpu
from jax.sharding import PartitionSpec as P

COL_TILE = 512
COUNT_TILE = 512
LAST_PARTS = 2


def after(x, *others):
    return lax.optimization_barrier((x,) + others)[0]


def in_hbm(x):
    return pltpu.with_memory_space_constraint(x, pltpu.MemorySpace.HBM)


def in_vmem(x):
    return pltpu.with_memory_space_constraint(x, pltpu.VMEM)


def count_kernel(dosage, missing, turned, sums, dosage_buf, missing_buf, sems):
    share, tile = dosage.shape
    step = min(COUNT_TILE, tile)
    parts = tile // step
    copies = []
    for j in range(parts):
        span = slice(j * step, (j + 1) * step)
        for i, (there, here) in enumerate(((dosage, dosage_buf), (missing, missing_buf))):
            copies.append(pltpu.make_async_copy(there.at[:, span], here.at[:, span], sems.at[2 * j + i]))
    for copy in copies:
        copy.start()
    alt = jnp.zeros((1, share), jnp.float32)
    obs = jnp.zeros((1, share), jnp.float32)
    for j in range(parts):
        span = slice(j * step, (j + 1) * step)
        copies[2 * j].wait()
        copies[2 * j + 1].wait()
        coded = jnp.where(missing_buf[:, span] == 0, dosage_buf[:, span], -1.0).T
        turned[span, :] = coded
        seen = coded >= 0.0
        alt += jnp.sum(jnp.where(seen, coded, 0.0), axis=0, keepdims=True)
        obs += jnp.sum(jnp.where(seen, 1.0, 0.0), axis=0, keepdims=True)
    sums[...] = jnp.concatenate([alt, obs, jnp.zeros((6, share), jnp.float32)], axis=0)


def count(dosage, missing):
    share, tile = dosage.shape
    anywhere = pl.BlockSpec(memory_space=pltpu.MemorySpace.HBM)
    vmem = pl.BlockSpec(memory_space=pltpu.VMEM)
    return pl.pallas_call(
        count_kernel,
        out_shape=(
            jax.ShapeDtypeStruct((tile, share), jnp.float32),
            jax.ShapeDtypeStruct((8, share), jnp.float32),
        ),
        in_specs=[anywhere, anywhere],
        out_specs=(vmem, vmem),
        scratch_shapes=[
            pltpu.VMEM((share, tile), jnp.float32),
            pltpu.VMEM((share, tile), jnp.int32),
            pltpu.SemaphoreType.DMA((2 * (tile // min(COUNT_TILE, tile)),)),
        ],
        compiler_params=pltpu.CompilerParams(vmem_limit_bytes=6 << 20),
    )(in_hbm(dosage), in_hbm(missing))


def standard_kernel(turned, sums, out):
    tile, share = turned.shape
    step = min(256, tile)
    freq = (sums[0:1, :] + 1.0) / (2.0 * sums[1:2, :] + 2.0)
    centre = 2.0 * freq
    scale = 1.0 / jnp.sqrt(2.0 * freq * (1.0 - freq))
    for j in range(tile // step):
        span = slice(j * step, (j + 1) * step)
        coded = turned[span, :]
        out[span, :] = jnp.where(coded >= 0.0, (coded - centre) * scale, 0.0).astype(out.dtype)


def standardise(turned, sums):
    vmem = pl.BlockSpec(memory_space=pltpu.VMEM)
    return pl.pallas_call(
        standard_kernel,
        out_shape=jax.ShapeDtypeStruct(turned.shape, jnp.bfloat16),
        in_specs=[vmem, vmem],
        out_specs=vmem,
        compiler_params=pltpu.CompilerParams(vmem_limit_bytes=4 << 20),
    )(in_vmem(turned), in_vmem(sums))


def slot_kernel(shift, n, ends, counts, place, row_all, col_all, grm, res, *refs):
    own_out, send_out, left_buf, total = refs[-4:]
    _, tile, share = row_all.shape
    chunk = tile // n
    col_tile = min(COL_TILE, tile)
    places, _, half = own_out.shape
    segments = counts.shape[0]
    group, col = place[0], place[1]
    own_at = pl.multiple_of(group * half, half)
    send_at = pl.multiple_of((1 - group) * half, half)
    first = pl.multiple_of(lax.rem(col + n - shift, n) * chunk, chunk)

    def segment(s, carry):
        if ends:
            which = jnp.where(s == 0, group * (segments - 1), segments - 2)
        else:
            which = s + 1
        own_count = counts[which]
        begins = lax.fori_loop(0, which, lambda i, total: total + counts[i], 0) - group * n * share
        lower = jnp.clip(begins, 0, n * share)
        upper = jnp.clip(begins + own_count, 0, n * share)
        first_piece = lower // share
        pieces = (upper + share - 1) // share - first_piece

        @pl.when(upper <= lower)
        def _():
            own_out[s] = jnp.zeros(own_out.shape[1:], own_out.dtype)
            send_out[s] = jnp.zeros(send_out.shape[1:], send_out.dtype)

        for m in range(1, n + 1):

            @pl.when((upper > lower) & (pieces == m))
            def _(m=m):
                lies = [lax.rem(col + n - first_piece - i, n) for i in range(m)]
                for i in range(m):
                    index = (first_piece + i) * share + lax.broadcasted_iota(
                        jnp.int32, (chunk, share), 1
                    )
                    left = row_all[lies[i], pl.ds(first, chunk), :]
                    left_buf[i] = jnp.where(
                        (index >= lower) & (index < upper), left, jnp.zeros_like(left)
                    )
                scale = 1.0 / jnp.full((1, col_tile), own_count, jnp.int32).astype(jnp.float32)
                for j in range(tile // col_tile):
                    span = slice(j * col_tile, (j + 1) * col_tile)
                    gram = None
                    for i in range(m):
                        part = lax.dot_general(
                            left_buf[i],
                            col_all[lies[i], span, :],
                            (((1,), (1,)), ((), ())),
                            preferred_element_type=jnp.float32,
                        )
                        gram = part if gram is None else gram + part
                    grm_part = grm[pl.ds(first, chunk), span].astype(jnp.float32)
                    hadamard = (gram * scale * grm_part).astype(jnp.bfloat16)
                    part = jnp.dot(hadamard, res[span, :], preferred_element_type=jnp.float32)
                    if j == 0:
                        total[...] = part
                    else:
                        total[...] += part
                own_out[s] = total[:, pl.ds(own_at, half)]
                send_out[s] = total[:, pl.ds(send_at, half)].astype(send_out.dtype)

        return carry

    lax.fori_loop(0, places, segment, 0)


def slot(shift, ends, counts, place, row_all, col_all, grm, res, earlier):
    n, tile, share = row_all.shape
    places = 2 if ends else counts.shape[0] - 3
    chunk = tile // n
    width = res.shape[1]
    half = width // 2
    smem = pl.BlockSpec(memory_space=pltpu.SMEM)
    vmem = pl.BlockSpec(memory_space=pltpu.VMEM)
    return pl.pallas_call(
        functools.partial(slot_kernel, shift, n, ends),
        out_shape=(
            jax.ShapeDtypeStruct((places, chunk, half), jnp.float32),
            jax.ShapeDtypeStruct((places, chunk, half), jnp.bfloat16),
        ),
        in_specs=[smem, smem, vmem, vmem, vmem, vmem]
        + [pl.BlockSpec(memory_space=pl.ANY)] * len(earlier),
        out_specs=(vmem, vmem),
        scratch_shapes=[
            pltpu.VMEM((n, chunk, share), jnp.bfloat16),
            pltpu.VMEM((chunk, width), jnp.float32),
        ],
        compiler_params=pltpu.CompilerParams(vmem_limit_bytes=8 << 20),
        cost_estimate=pl.CostEstimate(
            flops=2 * chunk * tile * (n * share + places * width),
            bytes_accessed=tile * n * share * 2 + chunk * tile * 2 + tile * width * 2,
            transcendentals=0,
        ),
    )(counts, place, in_vmem(row_all), in_vmem(col_all), in_vmem(grm), in_vmem(res), *earlier)


def shards(dosage, missing, residuals, global_grm, seg_counts):
    n_seg, n_row, n_col = (lax.axis_size(a) for a in ("segment", "row", "col"))
    assert n_seg == 2 and n_row == n_col
    group, row, col = (lax.axis_index(a) for a in ("segment", "row", "col"))
    segments = seg_counts.shape[0]
    share, tile = dosage.shape
    width = residuals.shape[1]
    half = width // 2
    half_vars = share * n_col
    bits = [1 << b for b in range(n_row.bit_length() - 1)]

    def spread(piece):
        have = piece
        for bit in reversed(bits):
            pairs = [
                (r * n_col + c, (r ^ bit) * n_col + c)
                for c in range(n_col)
                for r in range(n_row)
                if (r ^ c) & (2 * bit - 1) == 0
            ]
            got = lax.ppermute(have, ("row", "col"), pairs)
            have = jnp.where(((row ^ col) & (2 * bit - 1)) == bit, got, have)
        return have

    turned, sums = count(dosage, missing)
    for bit in bits:
        sums = sums + lax.ppermute(sums, "row", [(r, r ^ bit) for r in range(n_row)])
    standard = standardise(turned, sums)

    ring = [(i, (i + 1) % n_col) for i in range(n_col)]
    rows = [standard]
    cols = []
    res = None
    for s in range(1, n_col):
        piece = rows[-1]
        if s < n_col - 1:
            rows.append(lax.ppermute(piece, "col", ring))
            if s == 1:
                res = spread(after(residuals, standard))
            cols.append(spread(piece))
        else:
            part = tile // LAST_PARTS
            parts = [piece[i * part : (i + 1) * part] for i in range(LAST_PARTS)]
            last = [lax.ppermute(x, "col", ring) for x in parts]
            cols.append(spread(after(piece, *parts)))
            cols += [spread(last[0])] + [spread(after(x, cols[n_col - 2])) for x in last[1:]]
            rows += last
    row_all = jnp.concatenate(rows, axis=0).reshape(n_col, tile, share)
    col_all = jnp.concatenate(cols, axis=0).reshape(n_col, tile, share)

    place = jnp.stack([group, col]).astype(jnp.int32)
    swap = [(0, 1), (1, 0)]
    scores, crossing, sums = [], [], []

    def add_up(q):
        own, got = scores[q], crossing[q].astype(jnp.float32)
        if q % 2 == 0:
            got = jnp.concatenate([own[:1], own[1:] + got[1:], got[:1]], axis=0)
        else:
            got = own + got
        if q >= 2:
            got = got + lax.ppermute(sums[q - 2], "col", ring).astype(jnp.float32)
        sums.append(got.astype(jnp.bfloat16))

    for q in range(2 * n_col):
        if q >= 3:
            add_up(q - 3)
        own, send = slot(
            q // 2 + 1,
            q % 2 == 0,
            seg_counts,
            place,
            row_all,
            col_all,
            global_grm,
            res,
            scores[-1:] + sums[-1:],
        )
        scores.append(own)
        crossing.append(lax.ppermute(send, "segment", swap))
    for q in range(2 * n_col - 3, 2 * n_col):
        add_up(q)
    ends, middle = sums[-2:]
    ends = jnp.where(group == 0, ends, ends[::-1])
    return jnp.concatenate([ends[:1], middle, ends[1:]], axis=0)


def solution(mesh):
    placed = (
        P(("segment", "col"), "row"),
        P(("segment", "col"), "row"),
        P("row", None),
        P("row", "col"),
        P(),
    )
    return jax.shard_map(
        shards,
        mesh=mesh,
        in_specs=placed,
        out_specs=P(None, ("row", "col"), "segment"),
        check_vma=False,
    )
```

```python
import functools

import jax
import jax.numpy as jnp
from jax import lax
from jax.experimental import pallas as pl
from jax.experimental.pallas import tpu as pltpu
from jax.sharding import PartitionSpec as P

COL_TILE = 512
COUNT_TILE = 512
LAST_PARTS = 2


def after(x, *others):
    return lax.optimization_barrier((x,) + others)[0]


def in_hbm(x):
    return pltpu.with_memory_space_constraint(x, pltpu.MemorySpace.HBM)


def in_vmem(x):
    return pltpu.with_memory_space_constraint(x, pltpu.VMEM)


def count_kernel(dosage, missing, turned, sums, dosage_buf, missing_buf, sems):
    share, tile = dosage.shape
    step = min(COUNT_TILE, tile)
    parts = tile // step
    copies = []
    for j in range(parts):
        span = slice(j * step, (j + 1) * step)
        for i, (there, here) in enumerate(((dosage, dosage_buf), (missing, missing_buf))):
            copies.append(pltpu.make_async_copy(there.at[:, span], here.at[:, span], sems.at[2 * j + i]))
    for copy in copies:
        copy.start()
    alt = jnp.zeros((1, share), jnp.float32)
    obs = jnp.zeros((1, share), jnp.float32)
    for j in range(parts):
        span = slice(j * step, (j + 1) * step)
        copies[2 * j].wait()
        copies[2 * j + 1].wait()
        coded = jnp.where(missing_buf[:, span] == 0, dosage_buf[:, span], -1.0).T
        turned[span, :] = coded
        seen = coded >= 0.0
        alt += jnp.sum(jnp.where(seen, coded, 0.0), axis=0, keepdims=True)
        obs += jnp.sum(jnp.where(seen, 1.0, 0.0), axis=0, keepdims=True)
    sums[...] = jnp.concatenate([alt, obs, jnp.zeros((6, share), jnp.float32)], axis=0)


def count(dosage, missing):
    share, tile = dosage.shape
    anywhere = pl.BlockSpec(memory_space=pltpu.MemorySpace.HBM)
    vmem = pl.BlockSpec(memory_space=pltpu.VMEM)
    return pl.pallas_call(
        count_kernel,
        out_shape=(
            jax.ShapeDtypeStruct((tile, share), jnp.float32),
            jax.ShapeDtypeStruct((8, share), jnp.float32),
        ),
        in_specs=[anywhere, anywhere],
        out_specs=(vmem, vmem),
        scratch_shapes=[
            pltpu.VMEM((share, tile), jnp.float32),
            pltpu.VMEM((share, tile), jnp.int32),
            pltpu.SemaphoreType.DMA((2 * (tile // min(COUNT_TILE, tile)),)),
        ],
        compiler_params=pltpu.CompilerParams(vmem_limit_bytes=6 << 20),
    )(in_hbm(dosage), in_hbm(missing))


def standard_kernel(turned, sums, out):
    tile, share = turned.shape
    step = min(256, tile)
    freq = (sums[0:1, :] + 1.0) / (2.0 * sums[1:2, :] + 2.0)
    centre = 2.0 * freq
    scale = 1.0 / jnp.sqrt(2.0 * freq * (1.0 - freq))
    for j in range(tile // step):
        span = slice(j * step, (j + 1) * step)
        coded = turned[span, :]
        out[span, :] = jnp.where(coded >= 0.0, (coded - centre) * scale, 0.0).astype(out.dtype)


def standardise(turned, sums):
    vmem = pl.BlockSpec(memory_space=pltpu.VMEM)
    return pl.pallas_call(
        standard_kernel,
        out_shape=jax.ShapeDtypeStruct(turned.shape, jnp.bfloat16),
        in_specs=[vmem, vmem],
        out_specs=vmem,
        compiler_params=pltpu.CompilerParams(vmem_limit_bytes=4 << 20),
    )(in_vmem(turned), in_vmem(sums))


def slot_kernel(shift, n, ends, counts, place, row_all, col_all, grm, res, *refs):
    own_out, send_out, left_buf, total = refs[-4:]
    _, tile, share = row_all.shape
    chunk = tile // n
    col_tile = min(COL_TILE, tile)
    places, _, half = own_out.shape
    segments = counts.shape[0]
    group, col = place[0], place[1]
    own_at = pl.multiple_of(group * half, half)
    send_at = pl.multiple_of((1 - group) * half, half)
    first = pl.multiple_of(lax.rem(col + n - shift, n) * chunk, chunk)

    def segment(s, carry):
        if ends:
            which = jnp.where(s == 0, group * (segments - 1), segments - 2)
        else:
            which = s + 1
        own_count = counts[which]
        begins = lax.fori_loop(0, which, lambda i, total: total + counts[i], 0) - group * n * share
        lower = jnp.clip(begins, 0, n * share)
        upper = jnp.clip(begins + own_count, 0, n * share)
        first_piece = lower // share
        pieces = (upper + share - 1) // share - first_piece

        @pl.when(upper <= lower)
        def _():
            own_out[s] = jnp.zeros(own_out.shape[1:], own_out.dtype)
            send_out[s] = jnp.zeros(send_out.shape[1:], send_out.dtype)

        for m in range(1, n + 1):

            @pl.when((upper > lower) & (pieces == m))
            def _(m=m):
                lies = [lax.rem(col + n - first_piece - i, n) for i in range(m)]
                for i in range(m):
                    index = (first_piece + i) * share + lax.broadcasted_iota(
                        jnp.int32, (chunk, share), 1
                    )
                    left = row_all[lies[i], pl.ds(first, chunk), :]
                    left_buf[i] = jnp.where(
                        (index >= lower) & (index < upper), left, jnp.zeros_like(left)
                    )
                scale = 1.0 / jnp.full((1, col_tile), own_count, jnp.int32).astype(jnp.float32)
                for j in range(tile // col_tile):
                    span = slice(j * col_tile, (j + 1) * col_tile)
                    gram = None
                    for i in range(m):
                        part = lax.dot_general(
                            left_buf[i],
                            col_all[lies[i], span, :],
                            (((1,), (1,)), ((), ())),
                            preferred_element_type=jnp.float32,
                        )
                        gram = part if gram is None else gram + part
                    grm_part = grm[pl.ds(first, chunk), span].astype(jnp.float32)
                    hadamard = (gram * scale * grm_part).astype(jnp.bfloat16)
                    part = jnp.dot(hadamard, res[span, :], preferred_element_type=jnp.float32)
                    if j == 0:
                        total[...] = part
                    else:
                        total[...] += part
                own_out[s] = total[:, pl.ds(own_at, half)]
                send_out[s] = total[:, pl.ds(send_at, half)].astype(send_out.dtype)

        return carry

    lax.fori_loop(0, places, segment, 0)


def slot(shift, ends, counts, place, row_all, col_all, grm, res, earlier):
    n, tile, share = row_all.shape
    places = 2 if ends else counts.shape[0] - 3
    chunk = tile // n
    width = res.shape[1]
    half = width // 2
    smem = pl.BlockSpec(memory_space=pltpu.SMEM)
    vmem = pl.BlockSpec(memory_space=pltpu.VMEM)
    return pl.pallas_call(
        functools.partial(slot_kernel, shift, n, ends),
        out_shape=(
            jax.ShapeDtypeStruct((places, chunk, half), jnp.float32),
            jax.ShapeDtypeStruct((places, chunk, half), jnp.bfloat16),
        ),
        in_specs=[smem, smem, vmem, vmem, vmem, vmem]
        + [pl.BlockSpec(memory_space=pl.ANY)] * len(earlier),
        out_specs=(vmem, vmem),
        scratch_shapes=[
            pltpu.VMEM((n, chunk, share), jnp.bfloat16),
            pltpu.VMEM((chunk, width), jnp.float32),
        ],
        compiler_params=pltpu.CompilerParams(vmem_limit_bytes=8 << 20),
        cost_estimate=pl.CostEstimate(
            flops=2 * chunk * tile * (n * share + places * width),
            bytes_accessed=tile * n * share * 2 + chunk * tile * 2 + tile * width * 2,
            transcendentals=0,
        ),
    )(counts, place, in_vmem(row_all), in_vmem(col_all), in_vmem(grm), in_vmem(res), *earlier)


def shards(dosage, missing, residuals, global_grm, seg_counts):
    n_seg, n_row, n_col = (lax.axis_size(a) for a in ("segment", "row", "col"))
    assert n_seg == 2 and n_row == n_col
    group, row, col = (lax.axis_index(a) for a in ("segment", "row", "col"))
    segments = seg_counts.shape[0]
    share, tile = dosage.shape
    width = residuals.shape[1]
    half = width // 2
    half_vars = share * n_col
    bits = [1 << b for b in range(n_row.bit_length() - 1)]

    def hop(have, bit):
        pairs = [
            (r * n_col + c, (r ^ bit) * n_col + c)
            for c in range(n_col)
            for r in range(n_row)
            if (r ^ c) & (2 * bit - 1) == 0
        ]
        got = lax.ppermute(have, ("row", "col"), pairs)
        return jnp.where(((row ^ col) & (2 * bit - 1)) == bit, got, have)

    turned, sums = count(dosage, missing)
    for bit in bits:
        sums = sums + lax.ppermute(sums, "row", [(r, r ^ bit) for r in range(n_row)])
    standard = standardise(turned, sums)

    ring = [(i, (i + 1) % n_col) for i in range(n_col)]
    def spread(block):
        for bit in reversed(bits):
            block = hop(block, bit)
        return block

    rows, cols = [standard], []
    for i in range(n_col - 2):
        rows.append(lax.ppermute(rows[-1], "col", ring))
        if i == 0:
            res = spread(after(residuals, standard))
        cols.append(spread(rows[i]))
    part = tile // LAST_PARTS
    parts = [rows[-1][i * part : (i + 1) * part] for i in range(LAST_PARTS)]
    last = [lax.ppermute(x, "col", ring) for x in parts]
    cols.append(spread(after(rows[-1], *parts)))
    cols += [spread(x) for x in last]
    rows += last
    row_all = jnp.concatenate(rows, axis=0).reshape(n_col, tile, share)
    col_all = jnp.concatenate(cols, axis=0).reshape(n_col, tile, share)

    place = jnp.stack([group, col]).astype(jnp.int32)
    swap = [(0, 1), (1, 0)]
    scores, crossing, sums = [], [], []

    def add_up(q):
        own, got = scores[q], crossing[q].astype(jnp.float32)
        if q % 2 == 0:
            got = jnp.concatenate([own[:1], own[1:] + got[1:], got[:1]], axis=0)
        else:
            got = own + got
        if q >= 2:
            got = got + lax.ppermute(sums[q - 2], "col", ring).astype(jnp.float32)
        sums.append(got.astype(jnp.bfloat16))

    for q in range(2 * n_col):
        if q == 2:
            add_up(0)
        elif q >= 4:
            add_up(q - 3)
        own, send = slot(
            q // 2 + 1,
            q % 2 == 0,
            seg_counts,
            place,
            row_all,
            col_all,
            global_grm,
            res,
            scores[-1:] + sums[-1:],
        )
        scores.append(own)
        crossing.append(lax.ppermute(send, "segment", swap))
    for q in range(len(sums), 2 * n_col):
        add_up(q)
    ends, middle = sums[-2:]
    ends = jnp.where(group == 0, ends, ends[::-1])
    return jnp.concatenate([ends[:1], middle, ends[1:]], axis=0)


def solution(mesh):
    placed = (
        P(("segment", "col"), "row"),
        P(("segment", "col"), "row"),
        P("row", None),
        P("row", "col"),
        P(),
    )
    return jax.shard_map(
        shards,
        mesh=mesh,
        in_specs=placed,
        out_specs=P(None, ("row", "col"), "segment"),
        check_vma=False,
    )
```

```python
import functools

import jax
import jax.numpy as jnp
from jax import lax
from jax.experimental import pallas as pl
from jax.experimental.pallas import tpu as pltpu
from jax.sharding import PartitionSpec as P

COL_TILE = 512
COUNT_TILE = 512
LAST_PARTS = 2


def after(x, *others):
    return lax.optimization_barrier((x,) + others)[0]


def in_hbm(x):
    return pltpu.with_memory_space_constraint(x, pltpu.MemorySpace.HBM)


def in_vmem(x):
    return pltpu.with_memory_space_constraint(x, pltpu.VMEM)


def count_kernel(dosage, missing, turned, sums, dosage_buf, missing_buf, sems):
    share, tile = dosage.shape
    step = min(COUNT_TILE, tile)
    parts = tile // step
    copies = []
    for j in range(parts):
        span = slice(j * step, (j + 1) * step)
        for i, (there, here) in enumerate(((dosage, dosage_buf), (missing, missing_buf))):
            copies.append(pltpu.make_async_copy(there.at[:, span], here.at[:, span], sems.at[2 * j + i]))
    for copy in copies:
        copy.start()
    alt = jnp.zeros((1, share), jnp.float32)
    obs = jnp.zeros((1, share), jnp.float32)
    for j in range(parts):
        span = slice(j * step, (j + 1) * step)
        copies[2 * j].wait()
        copies[2 * j + 1].wait()
        coded = jnp.where(missing_buf[:, span] == 0, dosage_buf[:, span], -1.0).T
        turned[span, :] = coded
        seen = coded >= 0.0
        alt += jnp.sum(jnp.where(seen, coded, 0.0), axis=0, keepdims=True)
        obs += jnp.sum(jnp.where(seen, 1.0, 0.0), axis=0, keepdims=True)
    sums[...] = jnp.concatenate([alt, obs, jnp.zeros((6, share), jnp.float32)], axis=0)


def count(dosage, missing):
    share, tile = dosage.shape
    anywhere = pl.BlockSpec(memory_space=pltpu.MemorySpace.HBM)
    vmem = pl.BlockSpec(memory_space=pltpu.VMEM)
    return pl.pallas_call(
        count_kernel,
        out_shape=(
            jax.ShapeDtypeStruct((tile, share), jnp.float32),
            jax.ShapeDtypeStruct((8, share), jnp.float32),
        ),
        in_specs=[anywhere, anywhere],
        out_specs=(vmem, vmem),
        scratch_shapes=[
            pltpu.VMEM((share, tile), jnp.float32),
            pltpu.VMEM((share, tile), jnp.int32),
            pltpu.SemaphoreType.DMA((2 * (tile // min(COUNT_TILE, tile)),)),
        ],
        compiler_params=pltpu.CompilerParams(vmem_limit_bytes=6 << 20),
    )(in_hbm(dosage), in_hbm(missing))


def standard_kernel(turned, sums, out):
    tile, share = turned.shape
    step = min(256, tile)
    freq = (sums[0:1, :] + 1.0) / (2.0 * sums[1:2, :] + 2.0)
    centre = 2.0 * freq
    scale = 1.0 / jnp.sqrt(2.0 * freq * (1.0 - freq))
    for j in range(tile // step):
        span = slice(j * step, (j + 1) * step)
        coded = turned[span, :]
        out[span, :] = jnp.where(coded >= 0.0, (coded - centre) * scale, 0.0).astype(out.dtype)


def standardise(turned, sums):
    vmem = pl.BlockSpec(memory_space=pltpu.VMEM)
    return pl.pallas_call(
        standard_kernel,
        out_shape=jax.ShapeDtypeStruct(turned.shape, jnp.bfloat16),
        in_specs=[vmem, vmem],
        out_specs=vmem,
        compiler_params=pltpu.CompilerParams(vmem_limit_bytes=4 << 20),
    )(in_vmem(turned), in_vmem(sums))


def slot_kernel(shift, n, ends, counts, place, row_all, col_all, grm, res, *refs):
    own_out, send_out, left_buf, total = refs[-4:]
    _, tile, share = row_all.shape
    chunk = tile // n
    col_tile = min(COL_TILE, tile)
    places, _, half = own_out.shape
    segments = counts.shape[0]
    group, col = place[0], place[1]
    own_at = pl.multiple_of(group * half, half)
    send_at = pl.multiple_of((1 - group) * half, half)
    first = pl.multiple_of(lax.rem(col + n - shift, n) * chunk, chunk)

    def segment(s, carry):
        if ends:
            which = jnp.where(s == 0, group * (segments - 1), segments - 2)
        else:
            which = s + 1
        own_count = counts[which]
        begins = lax.fori_loop(0, which, lambda i, total: total + counts[i], 0) - group * n * share
        lower = jnp.clip(begins, 0, n * share)
        upper = jnp.clip(begins + own_count, 0, n * share)
        first_piece = lower // share
        pieces = (upper + share - 1) // share - first_piece

        @pl.when(upper <= lower)
        def _():
            own_out[s] = jnp.zeros(own_out.shape[1:], own_out.dtype)
            send_out[s] = jnp.zeros(send_out.shape[1:], send_out.dtype)

        for m in range(1, n + 1):

            @pl.when((upper > lower) & (pieces == m))
            def _(m=m):
                lies = [lax.rem(col + n - first_piece - i, n) for i in range(m)]
                for i in range(m):
                    index = (first_piece + i) * share + lax.broadcasted_iota(
                        jnp.int32, (chunk, share), 1
                    )
                    left = row_all[lies[i], pl.ds(first, chunk), :]
                    left_buf[i] = jnp.where(
                        (index >= lower) & (index < upper), left, jnp.zeros_like(left)
                    )
                scale = 1.0 / jnp.full((1, col_tile), own_count, jnp.int32).astype(jnp.float32)
                for j in range(tile // col_tile):
                    span = slice(j * col_tile, (j + 1) * col_tile)
                    gram = None
                    for i in range(m):
                        part = lax.dot_general(
                            left_buf[i],
                            col_all[lies[i], span, :],
                            (((1,), (1,)), ((), ())),
                            preferred_element_type=jnp.float32,
                        )
                        gram = part if gram is None else gram + part
                    grm_part = grm[pl.ds(first, chunk), span].astype(jnp.float32)
                    hadamard = (gram * scale * grm_part).astype(jnp.bfloat16)
                    part = jnp.dot(hadamard, res[span, :], preferred_element_type=jnp.float32)
                    if j == 0:
                        total[...] = part
                    else:
                        total[...] += part
                own_out[s] = total[:, pl.ds(own_at, half)]
                send_out[s] = total[:, pl.ds(send_at, half)].astype(send_out.dtype)

        return carry

    lax.fori_loop(0, places, segment, 0)


def slot(shift, ends, counts, place, row_all, col_all, grm, res, earlier):
    n, tile, share = row_all.shape
    places = 2 if ends else counts.shape[0] - 3
    chunk = tile // n
    width = res.shape[1]
    half = width // 2
    smem = pl.BlockSpec(memory_space=pltpu.SMEM)
    vmem = pl.BlockSpec(memory_space=pltpu.VMEM)
    return pl.pallas_call(
        functools.partial(slot_kernel, shift, n, ends),
        out_shape=(
            jax.ShapeDtypeStruct((places, chunk, half), jnp.float32),
            jax.ShapeDtypeStruct((places, chunk, half), jnp.bfloat16),
        ),
        in_specs=[smem, smem, vmem, vmem, vmem, vmem]
        + [pl.BlockSpec(memory_space=pl.ANY)] * len(earlier),
        out_specs=(vmem, vmem),
        scratch_shapes=[
            pltpu.VMEM((n, chunk, share), jnp.bfloat16),
            pltpu.VMEM((chunk, width), jnp.float32),
        ],
        compiler_params=pltpu.CompilerParams(vmem_limit_bytes=8 << 20),
        cost_estimate=pl.CostEstimate(
            flops=2 * chunk * tile * (n * share + places * width),
            bytes_accessed=tile * n * share * 2 + chunk * tile * 2 + tile * width * 2,
            transcendentals=0,
        ),
    )(counts, place, in_vmem(row_all), in_vmem(col_all), in_vmem(grm), in_vmem(res), *earlier)


def shards(dosage, missing, residuals, global_grm, seg_counts):
    n_seg, n_row, n_col = (lax.axis_size(a) for a in ("segment", "row", "col"))
    assert n_seg == 2 and n_row == n_col
    group, row, col = (lax.axis_index(a) for a in ("segment", "row", "col"))
    segments = seg_counts.shape[0]
    share, tile = dosage.shape
    width = residuals.shape[1]
    half = width // 2
    half_vars = share * n_col
    bits = [1 << b for b in range(n_row.bit_length() - 1)]

    def hop(have, bit):
        pairs = [
            (r * n_col + c, (r ^ bit) * n_col + c)
            for c in range(n_col)
            for r in range(n_row)
            if (r ^ c) & (2 * bit - 1) == 0
        ]
        got = lax.ppermute(have, ("row", "col"), pairs)
        return jnp.where(((row ^ col) & (2 * bit - 1)) == bit, got, have)

    turned, sums = count(dosage, missing)
    for bit in bits:
        sums = sums + lax.ppermute(sums, "row", [(r, r ^ bit) for r in range(n_row)])
    standard = standardise(turned, sums)

    ring = [(i, (i + 1) % n_col) for i in range(n_col)]
    def spread(block):
        for bit in reversed(bits):
            block = hop(block, bit)
        return block

    rows, cols = [standard], []
    for i in range(n_col - 2):
        rows.append(lax.ppermute(rows[-1], "col", ring))
        if i == 0:
            res = spread(after(residuals, rows[1]))
        cols.append(spread(rows[i]))
    part = tile // LAST_PARTS
    parts = [rows[-1][i * part : (i + 1) * part] for i in range(LAST_PARTS)]
    last = [lax.ppermute(x, "col", ring) for x in parts]
    cols.append(spread(after(rows[-1], *parts)))
    cols += [spread(x) for x in last]
    rows += last
    row_all = jnp.concatenate(rows, axis=0).reshape(n_col, tile, share)
    col_all = jnp.concatenate(cols, axis=0).reshape(n_col, tile, share)

    place = jnp.stack([group, col]).astype(jnp.int32)
    swap = [(0, 1), (1, 0)]
    scores, crossing, sums = [], [], []

    def add_up(q):
        own, got = scores[q], crossing[q].astype(jnp.float32)
        if q % 2 == 0:
            got = jnp.concatenate([own[:1], own[1:] + got[1:], got[:1]], axis=0)
        else:
            got = own + got
        if q >= 2:
            got = got + lax.ppermute(sums[q - 2], "col", ring).astype(jnp.float32)
        sums.append(got.astype(jnp.bfloat16))

    for q in range(2 * n_col):
        if q == 2:
            add_up(0)
        elif q >= 4:
            add_up(q - 3)
        own, send = slot(
            q // 2 + 1,
            q % 2 == 0,
            seg_counts,
            place,
            row_all,
            col_all,
            global_grm,
            res,
            scores[-1:] + sums[-1:],
        )
        scores.append(own)
        crossing.append(lax.ppermute(send, "segment", swap))
    for q in range(len(sums), 2 * n_col):
        add_up(q)
    ends, middle = sums[-2:]
    ends = jnp.where(group == 0, ends, ends[::-1])
    return jnp.concatenate([ends[:1], middle, ends[1:]], axis=0)


def solution(mesh):
    placed = (
        P(("segment", "col"), "row"),
        P(("segment", "col"), "row"),
        P("row", None),
        P("row", "col"),
        P(),
    )
    return jax.shard_map(
        shards,
        mesh=mesh,
        in_specs=placed,
        out_specs=P(None, ("row", "col"), "segment"),
        check_vma=False,
    )
```

```python
import functools

import jax
import jax.numpy as jnp
from jax import lax
from jax.experimental import pallas as pl
from jax.experimental.pallas import tpu as pltpu
from jax.sharding import PartitionSpec as P

COL_TILE = 512
COUNT_TILE = 512
LAST_PARTS = 2


def after(x, *others):
    return lax.optimization_barrier((x,) + others)[0]


def in_hbm(x):
    return pltpu.with_memory_space_constraint(x, pltpu.MemorySpace.HBM)


def in_vmem(x):
    return pltpu.with_memory_space_constraint(x, pltpu.VMEM)


def count_kernel(dosage, missing, turned, sums, dosage_buf, missing_buf, sems):
    share, tile = dosage.shape
    step = min(COUNT_TILE, tile)
    parts = tile // step
    copies = []
    for j in range(parts):
        span = slice(j * step, (j + 1) * step)
        for i, (there, here) in enumerate(((dosage, dosage_buf), (missing, missing_buf))):
            copies.append(pltpu.make_async_copy(there.at[:, span], here.at[:, span], sems.at[2 * j + i]))
    for copy in copies:
        copy.start()
    alt = jnp.zeros((1, share), jnp.float32)
    obs = jnp.zeros((1, share), jnp.float32)
    for j in range(parts):
        span = slice(j * step, (j + 1) * step)
        copies[2 * j].wait()
        copies[2 * j + 1].wait()
        coded = jnp.where(missing_buf[:, span] == 0, dosage_buf[:, span], -1.0).T
        turned[span, :] = coded
        seen = coded >= 0.0
        alt += jnp.sum(jnp.where(seen, coded, 0.0), axis=0, keepdims=True)
        obs += jnp.sum(jnp.where(seen, 1.0, 0.0), axis=0, keepdims=True)
    sums[...] = jnp.concatenate([alt, obs, jnp.zeros((6, share), jnp.float32)], axis=0)


def count(dosage, missing):
    share, tile = dosage.shape
    anywhere = pl.BlockSpec(memory_space=pltpu.MemorySpace.HBM)
    vmem = pl.BlockSpec(memory_space=pltpu.VMEM)
    return pl.pallas_call(
        count_kernel,
        out_shape=(
            jax.ShapeDtypeStruct((tile, share), jnp.float32),
            jax.ShapeDtypeStruct((8, share), jnp.float32),
        ),
        in_specs=[anywhere, anywhere],
        out_specs=(vmem, vmem),
        scratch_shapes=[
            pltpu.VMEM((share, tile), jnp.float32),
            pltpu.VMEM((share, tile), jnp.int32),
            pltpu.SemaphoreType.DMA((2 * (tile // min(COUNT_TILE, tile)),)),
        ],
        compiler_params=pltpu.CompilerParams(vmem_limit_bytes=6 << 20),
    )(in_hbm(dosage), in_hbm(missing))


def standard_kernel(turned, sums, out):
    tile, share = turned.shape
    step = min(256, tile)
    freq = (sums[0:1, :] + 1.0) / (2.0 * sums[1:2, :] + 2.0)
    centre = 2.0 * freq
    scale = 1.0 / jnp.sqrt(2.0 * freq * (1.0 - freq))
    for j in range(tile // step):
        span = slice(j * step, (j + 1) * step)
        coded = turned[span, :]
        out[span, :] = jnp.where(coded >= 0.0, (coded - centre) * scale, 0.0).astype(out.dtype)


def standardise(turned, sums):
    vmem = pl.BlockSpec(memory_space=pltpu.VMEM)
    return pl.pallas_call(
        standard_kernel,
        out_shape=jax.ShapeDtypeStruct(turned.shape, jnp.bfloat16),
        in_specs=[vmem, vmem],
        out_specs=vmem,
        compiler_params=pltpu.CompilerParams(vmem_limit_bytes=4 << 20),
    )(in_vmem(turned), in_vmem(sums))


def ring_place(col, n):
    return jnp.where(lax.rem(col, 2) == 0, col // 2, n - 1 - col // 2)


def ring_col(place, n):
    return jnp.where(2 * place < n, 2 * place, 2 * (n - 1 - place) + 1)


def slot_kernel(shift, n, ends, counts, place, row_all, col_all, grm, res, *refs):
    own_out, send_out, left_buf, total = refs[-4:]
    _, tile, share = row_all.shape
    chunk = tile // n
    col_tile = min(COL_TILE, tile)
    places, _, half = own_out.shape
    segments = counts.shape[0]
    group, here = place[0], ring_place(place[1], n)
    own_at = pl.multiple_of(group * half, half)
    send_at = pl.multiple_of((1 - group) * half, half)
    first = pl.multiple_of(ring_col(lax.rem(here + n - shift, n), n) * chunk, chunk)

    def segment(s, carry):
        if ends:
            which = jnp.where(s == 0, group * (segments - 1), segments - 2)
        else:
            which = s + 1
        own_count = counts[which]
        begins = lax.fori_loop(0, which, lambda i, total: total + counts[i], 0) - group * n * share
        lower = jnp.clip(begins, 0, n * share)
        upper = jnp.clip(begins + own_count, 0, n * share)
        first_piece = lower // share
        pieces = (upper + share - 1) // share - first_piece

        @pl.when(upper <= lower)
        def _():
            own_out[s] = jnp.zeros(own_out.shape[1:], own_out.dtype)
            send_out[s] = jnp.zeros(send_out.shape[1:], send_out.dtype)

        for m in range(1, n + 1):

            @pl.when((upper > lower) & (pieces == m))
            def _(m=m):
                lies = [lax.rem(here + n - ring_place(first_piece + i, n), n) for i in range(m)]
                for i in range(m):
                    index = (first_piece + i) * share + lax.broadcasted_iota(
                        jnp.int32, (chunk, share), 1
                    )
                    left = row_all[lies[i], pl.ds(first, chunk), :]
                    left_buf[i] = jnp.where(
                        (index >= lower) & (index < upper), left, jnp.zeros_like(left)
                    )
                scale = 1.0 / jnp.full((1, col_tile), own_count, jnp.int32).astype(jnp.float32)
                for j in range(tile // col_tile):
                    span = slice(j * col_tile, (j + 1) * col_tile)
                    gram = None
                    for i in range(m):
                        part = lax.dot_general(
                            left_buf[i],
                            col_all[lies[i], span, :],
                            (((1,), (1,)), ((), ())),
                            preferred_element_type=jnp.float32,
                        )
                        gram = part if gram is None else gram + part
                    grm_part = grm[pl.ds(first, chunk), span].astype(jnp.float32)
                    hadamard = (gram * scale * grm_part).astype(jnp.bfloat16)
                    part = jnp.dot(hadamard, res[span, :], preferred_element_type=jnp.float32)
                    if j == 0:
                        total[...] = part
                    else:
                        total[...] += part
                own_out[s] = total[:, pl.ds(own_at, half)]
                send_out[s] = total[:, pl.ds(send_at, half)].astype(send_out.dtype)

        return carry

    lax.fori_loop(0, places, segment, 0)


def slot(shift, ends, counts, place, row_all, col_all, grm, res, earlier):
    n, tile, share = row_all.shape
    places = 2 if ends else counts.shape[0] - 3
    chunk = tile // n
    width = res.shape[1]
    half = width // 2
    smem = pl.BlockSpec(memory_space=pltpu.SMEM)
    vmem = pl.BlockSpec(memory_space=pltpu.VMEM)
    return pl.pallas_call(
        functools.partial(slot_kernel, shift, n, ends),
        out_shape=(
            jax.ShapeDtypeStruct((places, chunk, half), jnp.float32),
            jax.ShapeDtypeStruct((places, chunk, half), jnp.bfloat16),
        ),
        in_specs=[smem, smem, vmem, vmem, vmem, vmem]
        + [pl.BlockSpec(memory_space=pl.ANY)] * len(earlier),
        out_specs=(vmem, vmem),
        scratch_shapes=[
            pltpu.VMEM((n, chunk, share), jnp.bfloat16),
            pltpu.VMEM((chunk, width), jnp.float32),
        ],
        compiler_params=pltpu.CompilerParams(vmem_limit_bytes=8 << 20),
        cost_estimate=pl.CostEstimate(
            flops=2 * chunk * tile * (n * share + places * width),
            bytes_accessed=tile * n * share * 2 + chunk * tile * 2 + tile * width * 2,
            transcendentals=0,
        ),
    )(counts, place, in_vmem(row_all), in_vmem(col_all), in_vmem(grm), in_vmem(res), *earlier)


def shards(dosage, missing, residuals, global_grm, seg_counts):
    n_seg, n_row, n_col = (lax.axis_size(a) for a in ("segment", "row", "col"))
    assert n_seg == 2 and n_row == n_col
    group, row, col = (lax.axis_index(a) for a in ("segment", "row", "col"))
    segments = seg_counts.shape[0]
    share, tile = dosage.shape
    width = residuals.shape[1]
    half = width // 2
    half_vars = share * n_col
    bits = [1 << b for b in range(n_row.bit_length() - 1)]

    def hop(have, bit):
        pairs = [
            (r * n_col + c, (r ^ bit) * n_col + c)
            for c in range(n_col)
            for r in range(n_row)
            if (r ^ c) & (2 * bit - 1) == 0
        ]
        got = lax.ppermute(have, ("row", "col"), pairs)
        return jnp.where(((row ^ col) & (2 * bit - 1)) == bit, got, have)

    turned, sums = count(dosage, missing)
    for bit in bits:
        sums = sums + lax.ppermute(sums, "row", [(r, r ^ bit) for r in range(n_row)])
    standard = standardise(turned, sums)

    order = [*range(0, n_col, 2), *range(n_col - 1 - n_col % 2, 0, -2)]
    ring = [(order[i - 1], order[i]) for i in range(n_col)]
    def spread(block):
        for bit in reversed(bits):
            block = hop(block, bit)
        return block

    rows, cols = [standard], []
    for i in range(n_col - 2):
        rows.append(lax.ppermute(rows[-1], "col", ring))
        if i == 0:
            res = spread(after(residuals, rows[1]))
        cols.append(spread(rows[i]))
    part = tile // LAST_PARTS
    parts = [rows[-1][i * part : (i + 1) * part] for i in range(LAST_PARTS)]
    last = [lax.ppermute(x, "col", ring) for x in parts]
    cols.append(spread(after(rows[-1], *parts)))
    cols += [spread(x) for x in last]
    rows += last
    row_all = jnp.concatenate(rows, axis=0).reshape(n_col, tile, share)
    col_all = jnp.concatenate(cols, axis=0).reshape(n_col, tile, share)

    place = jnp.stack([group, col]).astype(jnp.int32)
    swap = [(0, 1), (1, 0)]
    scores, crossing, sums = [], [], []

    def add_up(q):
        own, got = scores[q], crossing[q].astype(jnp.float32)
        if q % 2 == 0:
            got = jnp.concatenate([own[:1], own[1:] + got[1:], got[:1]], axis=0)
        else:
            got = own + got
        if q >= 2:
            got = got + lax.ppermute(sums[q - 2], "col", ring).astype(jnp.float32)
        sums.append(got.astype(jnp.bfloat16))

    for q in range(2 * n_col):
        if q == 2:
            add_up(0)
        elif q >= 4:
            add_up(q - 3)
        own, send = slot(
            q // 2 + 1,
            q % 2 == 0,
            seg_counts,
            place,
            row_all,
            col_all,
            global_grm,
            res,
            scores[-1:] + sums[-1:],
        )
        scores.append(own)
        crossing.append(lax.ppermute(send, "segment", swap))
    for q in range(len(sums), 2 * n_col):
        add_up(q)
    ends, middle = sums[-2:]
    ends = jnp.where(group == 0, ends, ends[::-1])
    return jnp.concatenate([ends[:1], middle, ends[1:]], axis=0)


def solution(mesh):
    placed = (
        P(("segment", "col"), "row"),
        P(("segment", "col"), "row"),
        P("row", None),
        P("row", "col"),
        P(),
    )
    return jax.shard_map(
        shards,
        mesh=mesh,
        in_specs=placed,
        out_specs=P(None, ("row", "col"), "segment"),
        check_vma=False,
    )
```

```python
import functools

import jax
import jax.numpy as jnp
from jax import lax
from jax.experimental import pallas as pl
from jax.experimental.pallas import tpu as pltpu
from jax.sharding import PartitionSpec as P

COL_TILE = 1536
COUNT_TILE = 512
LAST_PARTS = 2


def after(x, *others):
    return lax.optimization_barrier((x,) + others)[0]


def in_hbm(x):
    return pltpu.with_memory_space_constraint(x, pltpu.MemorySpace.HBM)


def in_vmem(x):
    return pltpu.with_memory_space_constraint(x, pltpu.VMEM)


def count_kernel(dosage, missing, turned, sums, dosage_buf, missing_buf, sems):
    share, tile = dosage.shape
    step = min(COUNT_TILE, tile)
    parts = tile // step
    copies = []
    for j in range(parts):
        span = slice(j * step, (j + 1) * step)
        for i, (there, here) in enumerate(((dosage, dosage_buf), (missing, missing_buf))):
            copies.append(pltpu.make_async_copy(there.at[:, span], here.at[:, span], sems.at[2 * j + i]))
    for copy in copies:
        copy.start()
    alt = jnp.zeros((1, share), jnp.float32)
    obs = jnp.zeros((1, share), jnp.float32)
    for j in range(parts):
        span = slice(j * step, (j + 1) * step)
        copies[2 * j].wait()
        copies[2 * j + 1].wait()
        coded = jnp.where(missing_buf[:, span] == 0, dosage_buf[:, span], -1.0).T
        turned[span, :] = coded
        seen = coded >= 0.0
        alt += jnp.sum(jnp.where(seen, coded, 0.0), axis=0, keepdims=True)
        obs += jnp.sum(jnp.where(seen, 1.0, 0.0), axis=0, keepdims=True)
    sums[...] = jnp.concatenate([alt, obs, jnp.zeros((6, share), jnp.float32)], axis=0)


def count(dosage, missing):
    share, tile = dosage.shape
    anywhere = pl.BlockSpec(memory_space=pltpu.MemorySpace.HBM)
    vmem = pl.BlockSpec(memory_space=pltpu.VMEM)
    return pl.pallas_call(
        count_kernel,
        out_shape=(
            jax.ShapeDtypeStruct((tile, share), jnp.float32),
            jax.ShapeDtypeStruct((8, share), jnp.float32),
        ),
        in_specs=[anywhere, anywhere],
        out_specs=(vmem, vmem),
        scratch_shapes=[
            pltpu.VMEM((share, tile), jnp.float32),
            pltpu.VMEM((share, tile), jnp.int32),
            pltpu.SemaphoreType.DMA((2 * (tile // min(COUNT_TILE, tile)),)),
        ],
        compiler_params=pltpu.CompilerParams(vmem_limit_bytes=6 << 20),
    )(in_hbm(dosage), in_hbm(missing))


def standard_kernel(turned, sums, out):
    tile, share = turned.shape
    step = min(256, tile)
    freq = (sums[0:1, :] + 1.0) / (2.0 * sums[1:2, :] + 2.0)
    centre = 2.0 * freq
    scale = 1.0 / jnp.sqrt(2.0 * freq * (1.0 - freq))
    for j in range(tile // step):
        span = slice(j * step, (j + 1) * step)
        coded = turned[span, :]
        out[span, :] = jnp.where(coded >= 0.0, (coded - centre) * scale, 0.0).astype(out.dtype)


def standardise(turned, sums):
    vmem = pl.BlockSpec(memory_space=pltpu.VMEM)
    return pl.pallas_call(
        standard_kernel,
        out_shape=jax.ShapeDtypeStruct(turned.shape, jnp.bfloat16),
        in_specs=[vmem, vmem],
        out_specs=vmem,
        compiler_params=pltpu.CompilerParams(vmem_limit_bytes=4 << 20),
    )(in_vmem(turned), in_vmem(sums))


def ring_place(col, n):
    return jnp.where(lax.rem(col, 2) == 0, col // 2, n - 1 - col // 2)


def ring_col(place, n):
    return jnp.where(2 * place < n, 2 * place, 2 * (n - 1 - place) + 1)


def slot_kernel(shift, n, ends, counts, place, row_all, col_all, grm, res, *refs):
    own_out, send_out, left_buf, total = refs[-4:]
    _, tile, share = row_all.shape
    chunk = tile // n
    col_tile = min(COL_TILE, tile)
    places, _, half = own_out.shape
    segments = counts.shape[0]
    group, here = place[0], ring_place(place[1], n)
    own_at = pl.multiple_of(group * half, half)
    send_at = pl.multiple_of((1 - group) * half, half)
    first = pl.multiple_of(ring_col(lax.rem(here + n - shift, n), n) * chunk, chunk)

    def segment(s, carry):
        if ends:
            which = jnp.where(s == 0, group * (segments - 1), segments - 2)
        else:
            which = s + 1
        own_count = counts[which]
        begins = lax.fori_loop(0, which, lambda i, total: total + counts[i], 0) - group * n * share
        lower = jnp.clip(begins, 0, n * share)
        upper = jnp.clip(begins + own_count, 0, n * share)
        first_piece = lower // share
        pieces = (upper + share - 1) // share - first_piece

        @pl.when(upper <= lower)
        def _():
            own_out[s] = jnp.zeros(own_out.shape[1:], own_out.dtype)
            send_out[s] = jnp.zeros(send_out.shape[1:], send_out.dtype)

        for m in range(1, n + 1):

            @pl.when((upper > lower) & (pieces == m))
            def _(m=m):
                lies = [lax.rem(here + n - ring_place(first_piece + i, n), n) for i in range(m)]
                for i in range(m):
                    index = (first_piece + i) * share + lax.broadcasted_iota(
                        jnp.int32, (chunk, share), 1
                    )
                    left = row_all[lies[i], pl.ds(first, chunk), :]
                    left_buf[:, i * share : (i + 1) * share] = jnp.where(
                        (index >= lower) & (index < upper), left, jnp.zeros_like(left)
                    )
                scale = 1.0 / jnp.full((1, col_tile), own_count, jnp.int32).astype(jnp.float32)
                for j in range(tile // col_tile):
                    span = slice(j * col_tile, (j + 1) * col_tile)
                    gram = lax.dot_general(
                        left_buf[:, : m * share],
                        jnp.concatenate([col_all[lies[i], span, :] for i in range(m)], axis=1),
                        (((1,), (1,)), ((), ())),
                        preferred_element_type=jnp.float32,
                    )
                    grm_part = grm[pl.ds(first, chunk), span].astype(jnp.float32)
                    hadamard = (gram * scale * grm_part).astype(jnp.bfloat16)
                    part = jnp.dot(hadamard, res[span, :], preferred_element_type=jnp.float32)
                    if j == 0:
                        total[...] = part
                    else:
                        total[...] += part
                own_out[s] = total[:, pl.ds(own_at, half)]
                send_out[s] = total[:, pl.ds(send_at, half)].astype(send_out.dtype)

        return carry

    lax.fori_loop(0, places, segment, 0)


def slot(shift, ends, counts, place, row_all, col_all, grm, res, earlier):
    n, tile, share = row_all.shape
    places = 2 if ends else counts.shape[0] - 3
    chunk = tile // n
    width = res.shape[1]
    half = width // 2
    smem = pl.BlockSpec(memory_space=pltpu.SMEM)
    vmem = pl.BlockSpec(memory_space=pltpu.VMEM)
    return pl.pallas_call(
        functools.partial(slot_kernel, shift, n, ends),
        out_shape=(
            jax.ShapeDtypeStruct((places, chunk, half), jnp.float32),
            jax.ShapeDtypeStruct((places, chunk, half), jnp.bfloat16),
        ),
        in_specs=[smem, smem, vmem, vmem, vmem, vmem]
        + [pl.BlockSpec(memory_space=pl.ANY)] * len(earlier),
        out_specs=(vmem, vmem),
        scratch_shapes=[
            pltpu.VMEM((chunk, n * share), jnp.bfloat16),
            pltpu.VMEM((chunk, width), jnp.float32),
        ],
        compiler_params=pltpu.CompilerParams(vmem_limit_bytes=8 << 20),
        cost_estimate=pl.CostEstimate(
            flops=2 * chunk * tile * (n * share + places * width),
            bytes_accessed=tile * n * share * 2 + chunk * tile * 2 + tile * width * 2,
            transcendentals=0,
        ),
    )(counts, place, in_vmem(row_all), in_vmem(col_all), in_vmem(grm), in_vmem(res), *earlier)


def shards(dosage, missing, residuals, global_grm, seg_counts):
    n_seg, n_row, n_col = (lax.axis_size(a) for a in ("segment", "row", "col"))
    assert n_seg == 2 and n_row == n_col
    group, row, col = (lax.axis_index(a) for a in ("segment", "row", "col"))
    segments = seg_counts.shape[0]
    share, tile = dosage.shape
    width = residuals.shape[1]
    half = width // 2
    half_vars = share * n_col
    bits = [1 << b for b in range(n_row.bit_length() - 1)]

    def hop(have, bit):
        pairs = [
            (r * n_col + c, (r ^ bit) * n_col + c)
            for c in range(n_col)
            for r in range(n_row)
            if (r ^ c) & (2 * bit - 1) == 0
        ]
        got = lax.ppermute(have, ("row", "col"), pairs)
        return jnp.where(((row ^ col) & (2 * bit - 1)) == bit, got, have)

    turned, sums = count(dosage, missing)
    for bit in bits:
        sums = sums + lax.ppermute(sums, "row", [(r, r ^ bit) for r in range(n_row)])
    standard = standardise(turned, sums)

    order = [*range(0, n_col, 2), *range(n_col - 1 - n_col % 2, 0, -2)]
    ring = [(order[i - 1], order[i]) for i in range(n_col)]
    def spread(block):
        for bit in reversed(bits):
            block = hop(block, bit)
        return block

    rows, cols = [standard], []
    for i in range(n_col - 2):
        rows.append(lax.ppermute(rows[-1], "col", ring))
        if i == 0:
            res = spread(after(residuals, rows[1]))
        cols.append(spread(rows[i]))
    part = tile // LAST_PARTS
    parts = [rows[-1][i * part : (i + 1) * part] for i in range(LAST_PARTS)]
    last = [lax.ppermute(x, "col", ring) for x in parts]
    cols.append(spread(after(rows[-1], *parts)))
    cols += [spread(x) for x in last]
    rows += last
    row_all = jnp.concatenate(rows, axis=0).reshape(n_col, tile, share)
    col_all = jnp.concatenate(cols, axis=0).reshape(n_col, tile, share)

    place = jnp.stack([group, col]).astype(jnp.int32)
    swap = [(0, 1), (1, 0)]
    scores, crossing, sums = [], [], []

    def add_up(q):
        own, got = scores[q], crossing[q].astype(jnp.float32)
        if q % 2 == 0:
            got = jnp.concatenate([own[:1], own[1:] + got[1:], got[:1]], axis=0)
        else:
            got = own + got
        if q >= 2:
            got = got + lax.ppermute(sums[q - 2], "col", ring).astype(jnp.float32)
        sums.append(got.astype(jnp.bfloat16))

    for q in range(2 * n_col):
        if q == 2:
            add_up(0)
        elif q >= 4:
            add_up(q - 3)
        own, send = slot(
            q // 2 + 1,
            q % 2 == 0,
            seg_counts,
            place,
            row_all,
            col_all,
            global_grm,
            res,
            scores[-1:] + sums[-1:],
        )
        scores.append(own)
        crossing.append(lax.ppermute(send, "segment", swap))
    for q in range(len(sums), 2 * n_col):
        add_up(q)
    ends, middle = sums[-2:]
    ends = jnp.where(group == 0, ends, ends[::-1])
    return jnp.concatenate([ends[:1], middle, ends[1:]], axis=0)


def solution(mesh):
    placed = (
        P(("segment", "col"), "row"),
        P(("segment", "col"), "row"),
        P("row", None),
        P("row", "col"),
        P(),
    )
    return jax.shard_map(
        shards,
        mesh=mesh,
        in_specs=placed,
        out_specs=P(None, ("row", "col"), "segment"),
        check_vma=False,
    )
```

```python
import functools

import jax
import jax.numpy as jnp
from jax import lax
from jax.experimental import pallas as pl
from jax.experimental.pallas import tpu as pltpu
from jax.sharding import PartitionSpec as P

COUNT_TILE = 512
LAST_PARTS = 2


def after(x, *others):
    return lax.optimization_barrier((x,) + others)[0]


def in_hbm(x):
    return pltpu.with_memory_space_constraint(x, pltpu.MemorySpace.HBM)


def in_vmem(x):
    return pltpu.with_memory_space_constraint(x, pltpu.VMEM)


def count_kernel(dosage, missing, turned, sums, dosage_buf, missing_buf, sems):
    share, tile = dosage.shape
    step = min(COUNT_TILE, tile)
    parts = tile // step
    copies = []
    for j in range(parts):
        span = slice(j * step, (j + 1) * step)
        for i, (there, here) in enumerate(((dosage, dosage_buf), (missing, missing_buf))):
            copies.append(pltpu.make_async_copy(there.at[:, span], here.at[:, span], sems.at[2 * j + i]))
    for copy in copies:
        copy.start()
    alt = jnp.zeros((1, share), jnp.float32)
    obs = jnp.zeros((1, share), jnp.float32)
    for j in range(parts):
        span = slice(j * step, (j + 1) * step)
        copies[2 * j].wait()
        copies[2 * j + 1].wait()
        coded = jnp.where(missing_buf[:, span] == 0, dosage_buf[:, span], -1.0).T
        turned[span, :] = coded
        seen = coded >= 0.0
        alt += jnp.sum(jnp.where(seen, coded, 0.0), axis=0, keepdims=True)
        obs += jnp.sum(jnp.where(seen, 1.0, 0.0), axis=0, keepdims=True)
    sums[...] = jnp.concatenate([alt, obs, jnp.zeros((6, share), jnp.float32)], axis=0)


def count(dosage, missing):
    share, tile = dosage.shape
    anywhere = pl.BlockSpec(memory_space=pltpu.MemorySpace.HBM)
    vmem = pl.BlockSpec(memory_space=pltpu.VMEM)
    return pl.pallas_call(
        count_kernel,
        out_shape=(
            jax.ShapeDtypeStruct((tile, share), jnp.float32),
            jax.ShapeDtypeStruct((8, share), jnp.float32),
        ),
        in_specs=[anywhere, anywhere],
        out_specs=(vmem, vmem),
        scratch_shapes=[
            pltpu.VMEM((share, tile), jnp.float32),
            pltpu.VMEM((share, tile), jnp.int32),
            pltpu.SemaphoreType.DMA((2 * (tile // min(COUNT_TILE, tile)),)),
        ],
        compiler_params=pltpu.CompilerParams(vmem_limit_bytes=6 << 20),
    )(in_hbm(dosage), in_hbm(missing))


def standard_kernel(turned, sums, out):
    tile, share = turned.shape
    step = min(256, tile)
    freq = (sums[0:1, :] + 1.0) / (2.0 * sums[1:2, :] + 2.0)
    centre = 2.0 * freq
    scale = 1.0 / jnp.sqrt(2.0 * freq * (1.0 - freq))
    for j in range(tile // step):
        span = slice(j * step, (j + 1) * step)
        coded = turned[span, :]
        out[span, :] = jnp.where(coded >= 0.0, (coded - centre) * scale, 0.0).astype(out.dtype)


def standardise(turned, sums):
    vmem = pl.BlockSpec(memory_space=pltpu.VMEM)
    return pl.pallas_call(
        standard_kernel,
        out_shape=jax.ShapeDtypeStruct(turned.shape, jnp.bfloat16),
        in_specs=[vmem, vmem],
        out_specs=vmem,
        compiler_params=pltpu.CompilerParams(vmem_limit_bytes=4 << 20),
    )(in_vmem(turned), in_vmem(sums))


def ring_place(col, n):
    return jnp.where(lax.rem(col, 2) == 0, col // 2, n - 1 - col // 2)


def ring_col(place, n):
    return jnp.where(2 * place < n, 2 * place, 2 * (n - 1 - place) + 1)


def slot_kernel(shift, n, ends, counts, place, row_all, col_all, grm, res, *refs):
    own_out, send_out, left_buf, hadamards, total, slots = refs[-6:]
    _, tile, share = row_all.shape
    chunk = tile // n
    places, _, half = own_out.shape
    segments = counts.shape[0]
    group, here = place[0], ring_place(place[1], n)
    own_at = pl.multiple_of(group * half, half)
    send_at = pl.multiple_of((1 - group) * half, half)
    first = pl.multiple_of(ring_col(lax.rem(here + n - shift, n), n) * chunk, chunk)

    def segment(s, carry):
        if ends:
            which = jnp.where(s == 0, group * (segments - 1), segments - 2)
        else:
            which = s + 1
        own_count = counts[which]
        begins = lax.fori_loop(0, which, lambda i, total: total + counts[i], 0) - group * n * share
        lower = jnp.clip(begins, 0, n * share)
        upper = jnp.clip(begins + own_count, 0, n * share)
        first_piece = lower // share
        pieces = (upper + share - 1) // share - first_piece

        @pl.when(upper <= lower)
        def _():
            own_out[s] = jnp.zeros(own_out.shape[1:], own_out.dtype)
            send_out[s] = jnp.zeros(send_out.shape[1:], send_out.dtype)

        for m in range(1, n + 1):

            @pl.when((upper > lower) & (pieces == m))
            def _(m=m):
                lies = [lax.rem(here + n - ring_place(first_piece + i, n), n) for i in range(m)]
                for i in range(m):
                    index = (first_piece + i) * share + lax.broadcasted_iota(
                        jnp.int32, (chunk, share), 1
                    )
                    left = row_all[lies[i], pl.ds(first, chunk), :]
                    left_buf[:, i * share : (i + 1) * share] = jnp.where(
                        (index >= lower) & (index < upper), left, jnp.zeros_like(left)
                    )
                scale = 1.0 / jnp.full((1, tile), own_count, jnp.int32).astype(jnp.float32)
                gram = lax.dot_general(
                    left_buf[:, : m * share],
                    jnp.concatenate([col_all[lies[i]] for i in range(m)], axis=1),
                    (((1,), (1,)), ((), ())),
                    preferred_element_type=jnp.float32,
                )
                grm_part = grm[pl.ds(first, chunk), :].astype(jnp.float32)
                at = pl.multiple_of(carry * chunk, chunk)
                hadamards[pl.ds(at, chunk), :] = (gram * scale * grm_part).astype(jnp.bfloat16)

        slots[s] = jnp.where(upper > lower, carry, -1)
        return carry + jnp.where(upper > lower, 1, 0)

    filled = lax.fori_loop(0, places, segment, jnp.int32(0))
    for m in range(1, places + 1):

        @pl.when(filled == m)
        def _(m=m):
            total[: m * chunk, :] = jnp.dot(
                hadamards[: m * chunk, :], res[...], preferred_element_type=jnp.float32
            )

    for s in range(places):

        @pl.when(slots[s] >= 0)
        def _(s=s):
            rows = pl.ds(pl.multiple_of(slots[s] * chunk, chunk), chunk)
            own_out[s] = total[rows, pl.ds(own_at, half)]
            send_out[s] = total[rows, pl.ds(send_at, half)].astype(send_out.dtype)


def slot(shift, ends, counts, place, row_all, col_all, grm, res, earlier):
    n, tile, share = row_all.shape
    places = 2 if ends else counts.shape[0] - 3
    chunk = tile // n
    width = res.shape[1]
    half = width // 2
    smem = pl.BlockSpec(memory_space=pltpu.SMEM)
    vmem = pl.BlockSpec(memory_space=pltpu.VMEM)
    return pl.pallas_call(
        functools.partial(slot_kernel, shift, n, ends),
        out_shape=(
            jax.ShapeDtypeStruct((places, chunk, half), jnp.float32),
            jax.ShapeDtypeStruct((places, chunk, half), jnp.bfloat16),
        ),
        in_specs=[smem, smem, vmem, vmem, vmem, vmem]
        + [pl.BlockSpec(memory_space=pl.ANY)] * len(earlier),
        out_specs=(vmem, vmem),
        scratch_shapes=[
            pltpu.VMEM((chunk, n * share), jnp.bfloat16),
            pltpu.VMEM((places * chunk, tile), jnp.bfloat16),
            pltpu.VMEM((places * chunk, width), jnp.float32),
            pltpu.SMEM((places,), jnp.int32),
        ],
        compiler_params=pltpu.CompilerParams(vmem_limit_bytes=14 << 20),
        cost_estimate=pl.CostEstimate(
            flops=2 * chunk * tile * (n * share + places * width),
            bytes_accessed=tile * n * share * 2 + chunk * tile * 2 + tile * width * 2,
            transcendentals=0,
        ),
    )(counts, place, in_vmem(row_all), in_vmem(col_all), in_vmem(grm), in_vmem(res), *earlier)


def shards(dosage, missing, residuals, global_grm, seg_counts):
    n_seg, n_row, n_col = (lax.axis_size(a) for a in ("segment", "row", "col"))
    assert n_seg == 2 and n_row == n_col
    group, row, col = (lax.axis_index(a) for a in ("segment", "row", "col"))
    segments = seg_counts.shape[0]
    share, tile = dosage.shape
    width = residuals.shape[1]
    half = width // 2
    half_vars = share * n_col
    bits = [1 << b for b in range(n_row.bit_length() - 1)]

    def hop(have, bit):
        pairs = [
            (r * n_col + c, (r ^ bit) * n_col + c)
            for c in range(n_col)
            for r in range(n_row)
            if (r ^ c) & (2 * bit - 1) == 0
        ]
        got = lax.ppermute(have, ("row", "col"), pairs)
        return jnp.where(((row ^ col) & (2 * bit - 1)) == bit, got, have)

    turned, sums = count(dosage, missing)
    for bit in bits:
        sums = sums + lax.ppermute(sums, "row", [(r, r ^ bit) for r in range(n_row)])
    standard = standardise(turned, sums)

    order = [*range(0, n_col, 2), *range(n_col - 1 - n_col % 2, 0, -2)]
    ring = [(order[i - 1], order[i]) for i in range(n_col)]
    def spread(block):
        for bit in reversed(bits):
            block = hop(block, bit)
        return block

    rows, cols = [standard], []
    for i in range(n_col - 2):
        rows.append(lax.ppermute(rows[-1], "col", ring))
        if i == 0:
            res = spread(after(residuals, rows[1]))
        cols.append(spread(rows[i]))
    part = tile // LAST_PARTS
    parts = [rows[-1][i * part : (i + 1) * part] for i in range(LAST_PARTS)]
    last = [lax.ppermute(x, "col", ring) for x in parts]
    cols.append(spread(after(rows[-1], *parts)))
    cols += [spread(x) for x in last]
    rows += last
    row_all = jnp.concatenate(rows, axis=0).reshape(n_col, tile, share)
    col_all = jnp.concatenate(cols, axis=0).reshape(n_col, tile, share)

    place = jnp.stack([group, col]).astype(jnp.int32)
    swap = [(0, 1), (1, 0)]
    scores, crossing, sums = [], [], []

    def add_up(q):
        own, got = scores[q], crossing[q].astype(jnp.float32)
        if q % 2 == 0:
            got = jnp.concatenate([own[:1], own[1:] + got[1:], got[:1]], axis=0)
        else:
            got = own + got
        if q >= 2:
            got = got + lax.ppermute(sums[q - 2], "col", ring).astype(jnp.float32)
        sums.append(got.astype(jnp.bfloat16))

    for q in range(2 * n_col):
        if q == 2:
            add_up(0)
        elif q >= 4:
            add_up(q - 3)
        own, send = slot(
            q // 2 + 1,
            q % 2 == 0,
            seg_counts,
            place,
            row_all,
            col_all,
            global_grm,
            res,
            scores[-1:] + sums[-1:],
        )
        scores.append(own)
        crossing.append(lax.ppermute(send, "segment", swap))
    for q in range(len(sums), 2 * n_col):
        add_up(q)
    ends, middle = sums[-2:]
    ends = jnp.where(group == 0, ends, ends[::-1])
    return jnp.concatenate([ends[:1], middle, ends[1:]], axis=0)


def solution(mesh):
    placed = (
        P(("segment", "col"), "row"),
        P(("segment", "col"), "row"),
        P("row", None),
        P("row", "col"),
        P(),
    )
    return jax.shard_map(
        shards,
        mesh=mesh,
        in_specs=placed,
        out_specs=P(None, ("row", "col"), "segment"),
        check_vma=False,
    )
```
